128 devices in a mesh: row: 8 (over z, x_lo), col: 8 (over y, x_hi), rep: 2 (over core).
Axes of the slice: x: 4 (x_hi: 2, x_lo: 2; x = x_hi * 2 + x_lo), y: 4, z: 4, core: 2. Of those that a mesh axis runs over, the one named last changes fastest.
Arguments:
- row_embed: float32 [8192, 512], P(('row', 'col')), may hold values from -1.2 to 1.2
- col_embed: float32 [512, 8192], P('row', 'col'), may hold values from -1.2 to 1.2
- counts: int32 [2, 16, 4096, 4096], P(None, 'rep', 'row', 'col'), may hold values from 0 to 192, as said below
- block_rows: int32 [2, 16, 8, 8], P(None, 'rep', 'row', 'col'), may hold values from 0 to 1
- block_cols: int32 [2, 16, 8, 8], P(None, 'rep', 'row', 'col'), may hold values from 0 to 1
- row_marginals: int32 [8192], P('row'), may hold values from 131072 to 6094848
- col_marginals: int32 [8192], P('col'), may hold values from 13107 to 406323
Outputs:
- new_row_embed: float32 [8192, 512], P(('row', 'col'))
- new_col_embed: float32 [512, 8192], P('row', 'col')
The draws below stay inside these ranges and needn't reach their ends.
Inputs may be any that keep to these rules, and one draw needn't show every extreme that they name: `counts`: zero in about a third of the entries.
All inputs are finite; a program needn't handle non-finite values.
Results may differ from the reference program's by a relative error of at most 0.0054.
Values may be sent and summed in bfloat16 or wider, within the bound.
No kernel may reach another device: no remote copies, remote signals or barrier semaphores. Data moves between devices by JAX's collectives and lax.ppermute only.
A program may use at most 128 MiB of HBM per device.

```python
import jax
import jax.numpy as jnp
from jax import lax

D = 512
BLK = 512
SLOTS = 8
GROUPS = 2
STEPS = 2
ROWS = 8192
COLS = 8192
N_ROW = 8
N_COL = 8
N_REP = 2


def draw_counts(key, part):
    key = jax.random.fold_in(key, 11)
    first, second = jax.random.split(key)
    shape = (STEPS, N_REP * SLOTS, N_ROW * BLK, N_COL * BLK)
    codes = jax.random.randint(first, shape, 0, 12)
    leading = jax.random.randint(second, shape, 1, 25)
    sizes = leading * jnp.left_shift(jnp.ones(shape, jnp.int32), codes // 3)
    return jnp.where(codes % 3 == 0, 0, sizes).astype(jnp.int32)


def draw_row_marginals(key, part):
    key = jax.random.fold_in(key, 23)
    first, second, third, fourth = jax.random.split(key, 4)
    slab = GROUPS * BLK
    leading = jax.random.randint(first, (ROWS,), 16, 32)
    power = jax.random.randint(second, (ROWS,), 0, 4)
    grid_row = jnp.arange(ROWS, dtype=jnp.int32) // slab
    factor = N_ROW - 1 + 2 * grid_row
    scaled = jnp.left_shift(leading, power) * factor // (N_ROW - 1)
    lowest = jax.random.randint(third, (), 0, slab)
    highest = jax.random.randint(fourth, (), ROWS - slab, ROWS)
    scaled = scaled.at[lowest].set(16).at[highest].set(744)
    return (scaled * COLS).astype(jnp.int32)


def draw_col_marginals(key, part):
    key = jax.random.fold_in(key, 37)
    first, second, third, fourth = jax.random.split(key, 4)
    leading = jax.random.randint(first, (COLS,), 16, 32)
    power = jax.random.randint(second, (COLS,), 0, 5)
    scaled = jnp.left_shift(leading, power)
    lowest = jax.random.randint(third, (), 0, COLS // 2)
    highest = jax.random.randint(fourth, (), COLS // 2, COLS)
    scaled = scaled.at[lowest].set(16).at[highest].set(496)
    return (scaled * ROWS // 10).astype(jnp.int32)


def set_ends(drawn, stream_key, low, largest):
    longest = drawn.shape.index(max(drawn.shape))
    spots = []
    for shift in (0, 1):
        where = [jax.random.randint(jax.random.fold_in(stream_key, axis), (), 0, length) for axis, length in enumerate(drawn.shape)]
        where[longest] = (where[longest] + shift) % drawn.shape[longest]
        spots.append(tuple(where))
    return drawn.at[spots[0]].set(low).at[spots[1]].set(largest)


def block_levels(own_key, extent, cuts, smallest, largest):
    level = 1.0
    for dim, blocks in cuts:
        draws = jax.random.uniform(jax.random.fold_in(jax.random.fold_in(own_key, 6), dim), (blocks,), jnp.float32, smallest / len(cuts), largest / len(cuts))
        level = level * jnp.repeat(jnp.exp(draws), extent[dim] // blocks).reshape((-1,) + (1,) * (len(extent) - 1 - dim))
    return level


def bell_draw(key, dims, spread, limit, cuts=(), held_as=jnp.bfloat16):
    factor_of = block_levels(key, dims, cuts, -0.22, 0.18) if cuts else 1.0
    entries = jax.random.normal(key, dims, jnp.float32) * spread * factor_of
    return jnp.minimum(jnp.maximum(entries, -limit), limit).astype(held_as)


def setup_inputs(seed: int = 0) -> dict:
    arg_keys = jax.random.split(jax.random.key(seed), 8)
    return {
        "row_embed": bell_draw(arg_keys[0], (ROWS, D), 0.2, 1.2, ((0, 64),), jnp.float32),
        "col_embed": bell_draw(arg_keys[1], (D, COLS), 0.2, 1.2, ((0, 8), (1, 8)), jnp.float32),
        "counts": draw_counts(jax.random.fold_in(arg_keys[7], 71), 0),
        "block_rows": set_ends(jax.random.randint(arg_keys[3], (STEPS, N_REP * SLOTS, N_ROW, N_COL), 0, GROUPS), jax.random.fold_in(arg_keys[3], 1), 0, GROUPS - 1).astype(jnp.int32),
        "block_cols": set_ends(jax.random.randint(arg_keys[4], (STEPS, N_REP * SLOTS, N_ROW, N_COL), 0, GROUPS), jax.random.fold_in(arg_keys[4], 1), 0, GROUPS - 1).astype(jnp.int32),
        "row_marginals": draw_row_marginals(jax.random.fold_in(arg_keys[7], 71), 0),
        "col_marginals": draw_col_marginals(jax.random.fold_in(arg_keys[7], 71), 0),
    }


def block_grad(dots, x, log_rows, log_cols, log_total):
    base = log_total - log_rows[:, None] - log_cols[None, :]
    xf = x.astype(jnp.float32)
    seen = x > 0
    weight = 0.1 + 0.25 * jnp.sqrt(xf)
    fitted = weight * (dots - jnp.log(jnp.maximum(xf, 1.0)) - base)
    hinge = jax.nn.sigmoid(dots - base)
    return jnp.where(seen, fitted, hinge).astype(jnp.bfloat16)

def reference(row_embed, col_embed, counts, block_rows, block_cols, row_marginals, col_marginals):
    log_total = jnp.log(jnp.sum(row_marginals.astype(jnp.float32)))
    log_rows = jnp.log(row_marginals.astype(jnp.float32))
    log_cols = jnp.log(col_marginals.astype(jnp.float32))
    slab = GROUPS * BLK
    cells = N_REP * SLOTS * N_ROW * N_COL
    order = jnp.arange(cells, dtype=jnp.int32)
    for step in range(STEPS):
        row_b = row_embed.astype(jnp.bfloat16)
        col_b = col_embed.astype(jnp.bfloat16)
        rows_step = block_rows[step].reshape(-1).astype(jnp.int32)
        cols_step = block_cols[step].reshape(-1).astype(jnp.int32)
        step_index = jnp.int32(step)

        def add_block(totals, index):
            row_grad, col_grad = totals
            slot = (index // (N_ROW * N_COL)).astype(jnp.int32)
            grid_r = (index // N_COL % N_ROW).astype(jnp.int32)
            grid_c = (index % N_COL).astype(jnp.int32)
            first_row = (grid_r * slab + rows_step[index] * BLK).astype(jnp.int32)
            first_col = (grid_c * slab + cols_step[index] * BLK).astype(jnp.int32)
            wblock = lax.dynamic_slice_in_dim(row_b, first_row, BLK, 0)
            cblock = lax.dynamic_slice_in_dim(col_b, first_col, BLK, 1)
            dots = jnp.dot(wblock, cblock, preferred_element_type=jnp.float32)
            starts = (step_index, slot, (grid_r * BLK).astype(jnp.int32), (grid_c * BLK).astype(jnp.int32))
            x = lax.dynamic_slice(counts, starts, (1, 1, BLK, BLK))[0, 0]
            grad = block_grad(dots, x, lax.dynamic_slice_in_dim(log_rows, first_row, BLK), lax.dynamic_slice_in_dim(log_cols, first_col, BLK), log_total)
            grad_w = jnp.dot(grad, cblock.T, preferred_element_type=jnp.float32)
            grad_c = jnp.dot(wblock.T, grad, preferred_element_type=jnp.float32)
            old_w = lax.dynamic_slice_in_dim(row_grad, first_row, BLK, 0)
            row_grad = lax.dynamic_update_slice_in_dim(row_grad, old_w + grad_w, first_row, 0)
            old_c = lax.dynamic_slice_in_dim(col_grad, first_col, BLK, 1)
            col_grad = lax.dynamic_update_slice_in_dim(col_grad, old_c + grad_c, first_col, 1)
            return ((row_grad, col_grad), index)
        empty_w = jnp.zeros(row_embed.shape, jnp.float32)
        empty_c = jnp.zeros(col_embed.shape, jnp.float32)
        (row_grad, col_grad), unused = lax.scan(add_block, (empty_w, empty_c), order)
        row_embed = row_embed - 0.002 * row_grad
        col_embed = col_embed - 0.002 * col_grad
    return (row_embed, col_embed)
```

```python
import functools

import jax
import jax.numpy as jnp
from jax import lax
from jax.experimental import pallas as pl
from jax.experimental.pallas import tpu as pltpu
from jax.sharding import PartitionSpec as P

RATE = 0.002
AXES = ("row", "col", "rep")
F32 = jnp.float32
BF16 = jnp.bfloat16
ABN_ROWS = 64
SUB = 16
NT = (((1,), (1,)), ((), ()))
TN = (((0,), (0,)), ((), ()))


def abn_kernel(rows, cols, x, a, b, n):
    for ref in (a, b, n):
        ref[...] = jnp.zeros(ref.shape, ref.dtype)

    def strip(i, carry):
        part = pl.ds(pl.multiple_of(i * SUB, SUB), SUB)
        for slot in range(x.shape[1]):
            xf = x[0, slot, part, :].astype(F32)
            seen = xf > 0
            top = jnp.maximum(xf, 1.0)
            weight = jnp.where(seen, 0.1 + 0.25 * (top * lax.rsqrt(top)), 0.0)
            at = (rows[slot], cols[slot], part, slice(None))
            a[at] += weight
            b[at] += weight * jnp.log(top)
            n[at] = (n[at].astype(F32) + jnp.where(seen, 0.0, 1.0)).astype(BF16)
        return carry

    lax.fori_loop(0, x.shape[2] // SUB, strip, 0)


def abn(counts, rows, cols, step):
    slots, block = counts.shape[1], counts.shape[2]
    out = pl.BlockSpec((2, 2, ABN_ROWS, block), lambda i, *_: (0, 0, i, 0))
    shape = (2, 2, block, block)
    return pl.pallas_call(
        abn_kernel,
        grid_spec=pltpu.PrefetchScalarGridSpec(
            num_scalar_prefetch=2,
            grid=(block // ABN_ROWS,),
            in_specs=[pl.BlockSpec((1, slots, ABN_ROWS, block), lambda i, *_: (step, 0, i, 0))],
            out_specs=[out, out, out],
        ),
        out_shape=[jax.ShapeDtypeStruct(shape, d) for d in (F32, F32, BF16)],
        compiler_params=pltpu.CompilerParams(vmem_limit_bytes=16 * 2**20),
        cost_estimate=pl.CostEstimate(flops=3 * 10**9, bytes_accessed=18 * 2**20, transcendentals=4 * 2**20),
        name="count_factors",
    )(rows, cols, counts)


def step_kernel(first, rep, own, other, a, b, n, lr, lc, *refs):
    if first:
        keep, send, log_total, grads = refs
    else:
        log_total, keep, send, grads = refs
    q = pl.program_id(0)

    def body(w, c, grad_w, grad_c):
        if first:

            @pl.when(q == 0)
            def _():
                pieces = c[:, 128:, :].astype(F32)
                log_total[...] = jnp.broadcast_to(
                    jnp.log(jnp.sum(pieces, axis=(0, 1), keepdims=False)[None, :]), log_total.shape
                )

        wq = w[pl.ds(2 * q, 2), :128, :].reshape(256, 512)
        row_part = lr[...]
        total = jnp.zeros((256, 512), F32)
        for h in range(2):
            ch = c[:, h * 64 : h * 64 + 64, :].reshape(512, 512)
            dots = jnp.dot(wq, ch, preferred_element_type=F32)
            t = dots + row_part + (lc[h] - log_total[0:1, :])
            hinge = 0.5 + 0.5 * jnp.tanh(0.5 * t)
            g = (t * a[0, h] - b[0, h] + n[0, h].astype(F32) * hinge).astype(BF16)
            grads[h, pl.ds(pl.multiple_of(q * 256, 256), 256), :] = g
            total += lax.dot_general(g, ch, NT, preferred_element_type=F32)
        grad_w[pl.ds(2 * q, 2)] = total.reshape(2, 128, 512).astype(grad_w.dtype)

        @pl.when(q == 3)
        def _():
            w_all = w[:, :128, :].reshape(1024, 512)
            for h in range(2):
                gc = lax.dot_general(w_all, grads[h], TN, preferred_element_type=F32)
                grad_c[:, h * 64 : h * 64 + 64, :] = gc.reshape(8, 64, 512).astype(grad_c.dtype)

    @pl.when(rep[0] == 0)
    def _():
        body(own, other, keep, send)

    @pl.when(rep[0] == 1)
    def _():
        body(other, own, send, keep)


def step_grads(rep, own, other, factors, lr, lc, log_total):
    first = log_total is None
    whole = lambda s: pl.BlockSpec(s, lambda q, *_: (0,) * len(s))
    quarter = pl.BlockSpec((1, 2, 256, 512), lambda q, *_: (q // 2, 0, q % 2, 0))
    in_specs = [whole(own.shape)] * 2 + [quarter] * 3 + [pl.BlockSpec((256, 1), lambda q, *_: (q, 0)), whole((2, 1, 512))]
    args = [rep, own, other, *factors, lr, lc]
    shape = (8, 128, 512)
    out_specs = [whole(shape)] * 2
    out_shape = [jax.ShapeDtypeStruct(shape, F32), jax.ShapeDtypeStruct(shape, BF16)]
    if first:
        out_specs.append(whole((8, 512)))
        out_shape.append(jax.ShapeDtypeStruct((8, 512), F32))
    else:
        in_specs.append(whole((8, 512)))
        args.append(log_total)
    return pl.pallas_call(
        functools.partial(step_kernel, first),
        grid_spec=pltpu.PrefetchScalarGridSpec(
            num_scalar_prefetch=1,
            grid=(4,),
            in_specs=in_specs,
            out_specs=out_specs,
            scratch_shapes=[pltpu.VMEM((2, 1024, 512), BF16)],
        ),
        out_shape=out_shape,
        compiler_params=pltpu.CompilerParams(vmem_limit_bytes=40 * 2**20),
        cost_estimate=pl.CostEstimate(flops=3 * 10**9, bytes_accessed=16 * 2**20, transcendentals=2**20),
        name="step_grads",
    )(*args)


def pieces_of(value):
    out = []
    for _ in range(3):
        top = lax.reduce_precision(value, 8, 7)
        out.append(top)
        value = value - top
    return jnp.stack(out + [jnp.zeros_like(value)] * 5).astype(BF16)


def per_device(groups, swap, row_embed, col_embed, counts, block_rows, block_cols, row_marginals, col_marginals):
    core = lax.axis_index("rep")
    is_w = core == 0
    rep = core.astype(jnp.int32).reshape(1)
    steps, slots = counts.shape[:2]

    def spread(x):
        return lax.all_to_all(x, AXES, 0, 0, axis_index_groups=groups, tiled=True)

    def other_core(x):
        return lax.ppermute(x, "rep", swap)

    packed_col = jnp.concatenate([col_embed[:, :512], col_embed[:, 512:]], axis=0)
    embed = jnp.where(is_w, row_embed, packed_col)
    row_f = row_marginals.astype(F32)
    extra = jnp.broadcast_to(pieces_of(jnp.sum(row_f))[:, None], (8, 512))
    lr = jnp.log(row_f)[:, None]
    lc = jnp.log(col_marginals.astype(F32)).reshape(2, 1, 512)
    rows = block_rows[:, :, 0, 0]
    cols = block_cols[:, :, 0, 0]

    log_total = None
    for step in range(steps):
        mine = embed.astype(BF16)
        if step == 0:
            mine = jnp.concatenate([mine, extra], axis=0)
        own = spread(jnp.broadcast_to(mine, (8,) + mine.shape))
        factors = abn(counts, rows[step], cols[step], step)
        other = other_core(own)
        res = step_grads(rep, own, other, factors, lr, lc, log_total)
        if step == 0:
            keep, send, log_total = res
        else:
            keep, send = res
        terms = (keep + other_core(send).astype(F32)).astype(BF16)
        share = spread(terms)
        embed = embed - RATE * jnp.sum(share.astype(F32), axis=0)
    theirs = other_core(embed)
    new_row = jnp.where(is_w, embed, theirs)
    new_col = jnp.where(is_w, theirs, embed)
    return new_row, jnp.concatenate([new_col[:64], new_col[64:]], axis=1)


def solution(mesh):
    n_row, n_col = mesh.shape["row"], mesh.shape["col"]
    index = lambda r, c, p: (r * n_col + c) * 2 + p
    groups = [[index(r, c, 0) for c in range(n_col)] for r in range(n_row)]
    groups += [[index(r, c, 1) for r in range(n_row)] for c in range(n_col)]
    swap = [(0, 1), (1, 0)]
    return jax.shard_map(
        functools.partial(per_device, groups, swap),
        mesh=mesh,
        in_specs=(
            P(("row", "col"), None),
            P("row", "col"),
            P(None, "rep", "row", "col"),
            P(None, "rep", "row", "col"),
            P(None, "rep", "row", "col"),
            P("row"),
            P("col"),
        ),
        out_specs=(P(("row", "col"), None), P("row", "col")),
        check_vma=False,
    )
```

```python
import functools

import jax
import jax.numpy as jnp
from jax import lax
from jax.experimental import pallas as pl
from jax.experimental.pallas import tpu as pltpu
from jax.sharding import PartitionSpec as P

RATE = 0.002
AXES = ("row", "col", "rep")
F32 = jnp.float32
BF16 = jnp.bfloat16
W_ROLE = 1
PIECE = 64
STRIP = 16
NT = (((1,), (1,)), ((), ()))
TN = (((0,), (0,)), ((), ()))
IN_VMEM = pl.BlockSpec(memory_space=pltpu.VMEM)
IN_HBM = pl.BlockSpec(memory_space=pltpu.HBM)
IN_SMEM = pl.BlockSpec(memory_space=pltpu.SMEM)


def vmem_kernel(kernel, mib, **kwargs):
    call = pl.pallas_call(kernel, compiler_params=pltpu.CompilerParams(vmem_limit_bytes=mib * 2**20), **kwargs)

    def run(*args):
        spaces = {id(IN_VMEM): pltpu.VMEM, id(IN_HBM): pltpu.HBM}
        return call(
            *(
                pltpu.with_memory_space_constraint(x, spaces[id(spec)]) if id(spec) in spaces else x
                for x, spec in zip(args, kwargs["in_specs"])
            )
        )

    return run


def abn_kernel(step, rows, cols, counts, a_out, b_out, n_out, done, held, a, b, n, seen, sem, out_sem):
    slots, block = counts.shape[1], counts.shape[2]

    def piece(i):
        return pltpu.make_async_copy(counts.at[step, :, pl.ds(i * PIECE, PIECE), :], held.at[i], sem.at[i])

    def result(i, k, ref, out):
        part = pl.ds(i * PIECE, PIECE)
        return pltpu.make_async_copy(ref.at[:, :, part, :], out.at[:, :, part, :], out_sem.at[i, k])

    results = [
        [result(i, k, ref, out) for k, (ref, out) in enumerate(((a, a_out), (b, b_out), (n, n_out)))]
        for i in range(block // PIECE)
    ]
    for i in range(block // PIECE):
        piece(i).start()
    for ref in (a, b, done, seen):
        ref[...] = jnp.zeros(ref.shape, F32)
    sampled = {}
    for g in range(2):
        for h in range(2):
            total = jnp.int32(0)
            for slot in range(slots):
                total += ((rows[slot] == g) & (cols[slot] == h)).astype(jnp.int32)
            sampled[g, h] = total.astype(F32)
    for i in range(block // PIECE):
        piece(i).wait()

        def strip(j, carry):
            here = pl.ds(pl.multiple_of(j * STRIP, STRIP), STRIP)
            part = pl.ds(pl.multiple_of(i * PIECE + j * STRIP, STRIP), STRIP)
            for slot in range(slots):
                xf = held[i, slot, here, :].astype(F32)
                top = jnp.maximum(xf, 1.0)
                root = xf * lax.rsqrt(top)
                at = (rows[slot], cols[slot], part, slice(None))
                a[at] += root
                b[at] += (0.1 + 0.25 * root) * jnp.log(top)
                seen[at] += jnp.minimum(xf, 1.0)
            for g in range(2):
                for h in range(2):
                    number = seen[g, h, part, :]
                    a[g, h, part, :] = 0.1 * number + 0.25 * a[g, h, part, :]
                    n[g, h, part, :] = (sampled[g, h] - number).astype(BF16)
            return carry

        lax.fori_loop(0, PIECE // STRIP, strip, 0)
        for copy in results[i]:
            copy.start()
    for copies in results:
        for copy in copies:
            copy.wait()


def abn(counts, rows, cols, step):
    slots, block = counts.shape[1], counts.shape[2]
    shape = (2, 2, block, block)
    return vmem_kernel(
        functools.partial(abn_kernel, step),
        28,
        in_specs=[IN_SMEM, IN_SMEM, IN_HBM],
        out_specs=[IN_HBM] * 3 + [IN_VMEM],
        out_shape=[pltpu.HBM(shape, d) for d in (F32, F32, BF16)] + [pltpu.VMEM((8, 128), F32)],
        scratch_shapes=[
            pltpu.VMEM((block // PIECE, slots, PIECE, block), jnp.int32),
            *(pltpu.VMEM(shape, d) for d in (F32, F32, BF16, F32)),
            pltpu.SemaphoreType.DMA((block // PIECE,)),
            pltpu.SemaphoreType.DMA((block // PIECE, 3)),
        ],
        cost_estimate=pl.CostEstimate(flops=6 * 10**9, bytes_accessed=8 * 2**20, transcendentals=4 * 2**20),
        name="count_factors",
    )(rows, cols, counts)


def step_kernel(first, role, own, other, a, b, n, lr, lc, *refs):
    if first:
        keep, send, log_total, grads = refs
    else:
        log_total, keep, send, grads = refs

    def body(w, c, grad_w, grad_c):
        if first:
            pieces = c[:, 128:, :].astype(F32)
            log_total[...] = jnp.broadcast_to(
                jnp.log(jnp.sum(pieces, axis=(0, 1), keepdims=False)[None, :]), log_total.shape
            )
        for g in range(2):
            wg = w[4 * g : 4 * g + 4, :128, :].reshape(512, 512)
            total = None
            for h in range(2):
                ch = c[:, h * 64 : h * 64 + 64, :].reshape(512, 512)
                dots = jnp.dot(wg, ch, preferred_element_type=F32)
                t = dots + lr[g * 512 : g * 512 + 512, :] + (lc[h] - log_total[0:1, :])
                hinge = 0.5 + 0.5 * jnp.tanh(0.5 * t)
                grad = (t * a[g, h] - b[g, h] + n[g, h].astype(F32) * hinge).astype(BF16)
                grads[h, g * 512 : g * 512 + 512, :] = grad
                term = lax.dot_general(grad, ch, NT, preferred_element_type=F32)
                total = term if total is None else total + term
            grad_w[4 * g : 4 * g + 4] = total.reshape(4, 128, 512).astype(grad_w.dtype)
        w_all = w[:, :128, :].reshape(1024, 512)
        for h in range(2):
            term = lax.dot_general(w_all, grads[h], TN, preferred_element_type=F32)
            grad_c[:, h * 64 : h * 64 + 64, :] = term.reshape(8, 64, 512).astype(grad_c.dtype)

    @pl.when(role[0] == W_ROLE)
    def _():
        body(own, other, keep, send)

    @pl.when(role[0] != W_ROLE)
    def _():
        body(other, own, send, keep)


def step_grads(role, own, other, factors, lr, lc, log_total):
    first = log_total is None
    args = [role, own, other, *factors, lr, lc] + ([] if first else [log_total])
    shape = (8, 128, 512)
    out_shape = [pltpu.VMEM(shape, F32), pltpu.VMEM(shape, BF16)] + ([pltpu.VMEM((8, 512), F32)] if first else [])
    return vmem_kernel(
        functools.partial(step_kernel, first),
        24,
        in_specs=[IN_SMEM] + [IN_VMEM] * (len(args) - 1),
        out_specs=[IN_VMEM] * len(out_shape),
        out_shape=out_shape,
        scratch_shapes=[pltpu.VMEM((2, 1024, 512), BF16)],
        cost_estimate=pl.CostEstimate(flops=3 * 10**9, bytes_accessed=16 * 2**20, transcendentals=2**20),
        name="step_grads",
    )(*args)


def load_kernel(done, *refs):
    *ins_outs, sem = refs
    copies = [
        pltpu.make_async_copy(ins_outs[k].at[g, h], ins_outs[k + 3].at[g, h], sem.at[2 * g + h, k])
        for g in range(2)
        for h in range(2)
        for k in range(3)
    ]
    for copy in copies:
        copy.start()
    for copy in copies:
        copy.wait()


def load(done, factors):
    return vmem_kernel(
        load_kernel,
        2,
        in_specs=[IN_VMEM] + [IN_HBM] * 3,
        out_specs=[IN_VMEM] * 3,
        out_shape=[pltpu.VMEM(x.shape, x.dtype) for x in factors],
        scratch_shapes=[pltpu.SemaphoreType.DMA((4, 3))],
        cost_estimate=pl.CostEstimate(flops=0, bytes_accessed=20 * 2**20, transcendentals=0),
        name="load_factors",
    )(done, *factors)


def update_kernel(share, embed, new, payload=None, chunk=None, sem=None):
    total = share[0].astype(F32)
    for k in range(1, 8):
        total += share[k].astype(F32)
    fresh = embed[...] - RATE * total
    new[...] = fresh
    if payload is not None:
        chunk[...] = fresh.astype(BF16)
        copy_to_all(chunk, payload, sem)


def update(share, embed, last):
    more = not last
    return vmem_kernel(
        update_kernel,
        4,
        in_specs=[IN_VMEM] * 2,
        out_specs=[IN_VMEM] + [IN_HBM] * more,
        out_shape=[pltpu.VMEM(embed.shape, F32)] + [pltpu.HBM(share.shape, BF16)] * more,
        scratch_shapes=[pltpu.VMEM(embed.shape, BF16), pltpu.SemaphoreType.DMA((8,))] * more,
        name="update",
    )(share, embed)


def prep_kernel(role, row_embed, col_embed, marginals, embed, payload, sums, chunk, sem):
    sum_copy = pltpu.make_async_copy(marginals, sums, sem.at[0])
    sum_copy.start()

    @pl.when(role[0] == W_ROLE)
    def _():
        copy = pltpu.make_async_copy(row_embed, embed, sem.at[1])
        copy.start()
        copy.wait()

    @pl.when(role[0] != W_ROLE)
    def _():
        low = pltpu.make_async_copy(col_embed.at[:, pl.ds(0, 512)], embed.at[pl.ds(0, 64)], sem.at[1])
        high = pltpu.make_async_copy(col_embed.at[:, pl.ds(512, 512)], embed.at[pl.ds(64, 64)], sem.at[2])
        low.start()
        high.start()
        low.wait()
        high.wait()

    sum_copy.wait()
    mine = embed[...].astype(BF16)
    rest = jnp.sum(sums[...].astype(F32), axis=(0, 1), keepdims=True)
    line = lax.broadcasted_iota(jnp.int32, (8, 512), 0)
    extra = jnp.zeros((8, 512), F32)
    for k in range(3):
        piece = rest.astype(BF16).astype(F32)
        extra = jnp.where(line == k, piece, extra)
        rest = rest - piece
    chunk[:128, :] = mine
    chunk[128:, :] = extra.astype(BF16)
    copy_to_all(chunk, payload, sem)


def copy_to_all(chunk, payload, sem):
    copies = [pltpu.make_async_copy(chunk, payload.at[k], sem.at[k]) for k in range(8)]
    for copy in copies:
        copy.start()
    for copy in copies:
        copy.wait()


def prep(role, row_embed, col_embed, marginals):
    return vmem_kernel(
        prep_kernel,
        4,
        in_specs=[IN_SMEM, IN_HBM, IN_HBM, IN_HBM],
        out_specs=[IN_VMEM, IN_HBM],
        out_shape=[pltpu.VMEM((128, 512), F32), pltpu.HBM((8, 136, 512), BF16)],
        scratch_shapes=[
            pltpu.VMEM((8, 128), jnp.int32),
            pltpu.VMEM((136, 512), BF16),
            pltpu.SemaphoreType.DMA((8,)),
        ],
        name="first_payload",
    )(role, row_embed, col_embed, marginals.reshape(8, 128))


def finish_kernel(role, embed, theirs, new_row, new_col, sem):
    def write(row, col):
        copies = [
            pltpu.make_async_copy(row, new_row, sem.at[0]),
            pltpu.make_async_copy(col.at[pl.ds(0, 64)], new_col.at[:, pl.ds(0, 512)], sem.at[1]),
            pltpu.make_async_copy(col.at[pl.ds(64, 64)], new_col.at[:, pl.ds(512, 512)], sem.at[2]),
        ]
        for copy in copies:
            copy.start()
        for copy in copies:
            copy.wait()

    @pl.when(role[0] == W_ROLE)
    def _():
        write(embed, theirs)

    @pl.when(role[0] != W_ROLE)
    def _():
        write(theirs, embed)


def finish(role, embed, theirs):
    return vmem_kernel(
        finish_kernel,
        4,
        in_specs=[IN_SMEM, IN_VMEM, IN_VMEM],
        out_specs=[IN_HBM] * 2,
        out_shape=[pltpu.HBM((128, 512), F32), pltpu.HBM((64, 1024), F32)],
        scratch_shapes=[pltpu.SemaphoreType.DMA((3,))],
        name="results",
    )(role, embed, theirs)


def per_device(groups, swap, row_embed, col_embed, counts, block_rows, block_cols, row_marginals, col_marginals):
    role = lax.axis_index("rep").astype(jnp.int32).reshape(1)
    steps = counts.shape[0]

    def spread(x):
        return lax.all_to_all(x, AXES, 0, 0, axis_index_groups=groups, tiled=True)

    def other_core(x):
        return lax.ppermute(x, "rep", swap)

    embed, payload = prep(role, row_embed, col_embed, row_marginals)
    payload, block_rows, block_cols, row_marginals, col_marginals = lax.optimization_barrier(
        (payload, block_rows, block_cols, row_marginals, col_marginals)
    )
    lr = jnp.log(row_marginals.astype(F32))[:, None]
    lc = jnp.log(col_marginals.astype(F32)).reshape(2, 1, 512)
    rows = block_rows[:, :, 0, 0]
    cols = block_cols[:, :, 0, 0]

    log_total = None
    for step in range(steps):
        last = step + 1 == steps
        payload, rows, cols = lax.optimization_barrier((payload, rows, cols))
        own = spread(payload)
        *factors, done = abn(counts, rows[step], cols[step], step)
        own, done = lax.optimization_barrier((own, done))
        other = other_core(own)
        factors = load(done, factors)
        res = step_grads(role, own, other, factors, lr, lc, log_total)
        if step == 0:
            keep, send, log_total = res
        else:
            keep, send = res
        terms = (keep + other_core(send).astype(F32)).astype(BF16)
        res = update(spread(terms), embed, last)
        if last:
            (embed,) = res
        else:
            embed, payload = res
    return tuple(finish(role, embed, other_core(embed)))


def solution(mesh):
    n_row, n_col = mesh.shape["row"], mesh.shape["col"]
    index = lambda r, c, p: (r * n_col + c) * 2 + p
    groups = [[index(r, c, W_ROLE) for c in range(n_col)] for r in range(n_row)]
    groups += [[index(r, c, 1 - W_ROLE) for r in range(n_row)] for c in range(n_col)]
    swap = [(0, 1), (1, 0)]
    return jax.shard_map(
        functools.partial(per_device, groups, swap),
        mesh=mesh,
        in_specs=(
            P(("row", "col"), None),
            P("row", "col"),
            P(None, "rep", "row", "col"),
            P(None, "rep", "row", "col"),
            P(None, "rep", "row", "col"),
            P("row"),
            P("col"),
        ),
        out_specs=(P(("row", "col"), None), P("row", "col")),
        check_vma=False,
    )
```

```python
import functools

import jax
import jax.numpy as jnp
from jax import lax
from jax.experimental import pallas as pl
from jax.experimental.pallas import tpu as pltpu
from jax.sharding import PartitionSpec as P

RATE = 0.002
AXES = ("row", "col", "rep")
F32 = jnp.float32
BF16 = jnp.bfloat16
W_ROLE = 1
PIECE = 64
STRIP = 16
NT = (((1,), (1,)), ((), ()))
TN = (((0,), (0,)), ((), ()))
IN_VMEM = pl.BlockSpec(memory_space=pltpu.VMEM)
IN_HBM = pl.BlockSpec(memory_space=pltpu.HBM)
IN_SMEM = pl.BlockSpec(memory_space=pltpu.SMEM)


def vmem_kernel(kernel, mib, **kwargs):
    call = pl.pallas_call(kernel, compiler_params=pltpu.CompilerParams(vmem_limit_bytes=mib * 2**20), **kwargs)

    def run(*args):
        spaces = {id(IN_VMEM): pltpu.VMEM, id(IN_HBM): pltpu.HBM}
        return call(
            *(
                pltpu.with_memory_space_constraint(x, spaces[id(spec)]) if id(spec) in spaces else x
                for x, spec in zip(args, kwargs["in_specs"])
            )
        )

    return run


def place(here):
    i = here[0]
    col, row = (i >> 1) & 7, i >> 4
    return i & 1, (col >> 1, col & 1), (row >> 1, row & 1)


def own_place(here):
    role, of_w, of_c = place(here)
    return [jnp.where(role == W_ROLE, p, q) for p, q in zip(of_w, of_c)]


def abn_kernel(step, half, rows, cols, counts, a, b, n, done, held, seen, sem):
    slots, extent = counts.shape[1], counts.shape[2] // 2

    def piece(i):
        part = pl.ds(half * extent + i * PIECE, PIECE)
        return pltpu.make_async_copy(counts.at[step, :, part, :], held.at[i], sem.at[i])

    for i in range(extent // PIECE):
        piece(i).start()
    for ref in (a, b, done, seen):
        ref[...] = jnp.zeros(ref.shape, F32)
    sampled = {}
    for g in range(2):
        for h in range(2):
            total = jnp.int32(0)
            for slot in range(slots):
                total += ((rows[step, slot] == g) & (cols[step, slot] == h)).astype(jnp.int32)
            sampled[g, h] = total.astype(F32)
    for i in range(extent // PIECE):
        piece(i).wait()

        def strip(j, carry):
            here = pl.ds(pl.multiple_of(j * STRIP, STRIP), STRIP)
            part = pl.ds(pl.multiple_of(i * PIECE + j * STRIP, STRIP), STRIP)
            for slot in range(slots):
                xf = held[i, slot, here, :].astype(F32)
                top = jnp.maximum(xf, 1.0)
                root = xf * lax.rsqrt(top)
                at = (rows[step, slot], cols[step, slot], part, slice(None))
                a[at] += root
                b[at] += (0.1 + 0.25 * root) * jnp.log(top)
                seen[at] += jnp.minimum(xf, 1.0)
            for g in range(2):
                for h in range(2):
                    number = seen[g, h, part, :]
                    a[g, h, part, :] = 0.1 * number + 0.25 * a[g, h, part, :]
                    n[g, h, part, :] = (sampled[g, h] - number).astype(BF16)
            return carry

        lax.fori_loop(0, PIECE // STRIP, strip, 0)


def abn(counts, rows, cols, step, half):
    slots, block = counts.shape[1], counts.shape[2]
    shape = (2, 2, block // 2, block)
    pieces = block // 2 // PIECE
    *factors, done = vmem_kernel(
        functools.partial(abn_kernel, step, half),
        8,
        in_specs=[IN_SMEM, IN_SMEM, IN_HBM],
        out_specs=[IN_VMEM] * 4,
        out_shape=[pltpu.VMEM(shape, d) for d in (F32, F32, BF16)] + [pltpu.VMEM((8, 128), F32)],
        scratch_shapes=[
            pltpu.VMEM((pieces, slots, PIECE, block), jnp.int32),
            pltpu.VMEM(shape, F32),
            pltpu.SemaphoreType.DMA((pieces,)),
        ],
        cost_estimate=pl.CostEstimate(flops=3 * 10**9, bytes_accessed=4 * 2**20, transcendentals=2 * 2**20),
        name="count_factors",
    )(rows, cols, counts)
    return factors, done


def front_kernel(first, here, own_a, own_b, other_a, other_b, *refs):
    a, b, n = refs[0:6:3], refs[1:6:3], refs[2:6:3]
    lr, lc, *refs = refs[6:]
    if first:
        w, c, grads, send, log_total = refs
    else:
        log_total, w, c, grads, send = refs
    role, (_, ws), (_, cs) = place(here)

    def assemble(w_a, w_b, c_a, c_b):
        for k in range(4):
            w[2 * k + ws] = w_a[k, :128, :]
            w[2 * k + 1 - ws] = w_b[k, :128, :]
            c[2 * k + cs] = c_a[k, :128, :]
            c[2 * k + 1 - cs] = c_b[k, :128, :]
        if first:
            pieces = c_a[:, 128:, :].astype(F32) + c_b[:, 128:, :].astype(F32)
            log_total[...] = jnp.broadcast_to(
                jnp.log(jnp.sum(pieces, axis=(0, 1), keepdims=False)[None, :]), log_total.shape
            )

    @pl.when(role == W_ROLE)
    def _():
        assemble(own_a, own_b, other_a, other_b)

    @pl.when(role != W_ROLE)
    def _():
        assemble(other_a, other_b, own_a, own_b)

    for g in range(2):
        wg = w[4 * g : 4 * g + 4].reshape(512, 512)
        for h in range(2):
            ch = c[:, h * 64 : h * 64 + 64, :].reshape(512, 512)
            dots = jnp.dot(wg, ch, preferred_element_type=F32)
            t = dots + jnp.tile(lr[g * 512 : g * 512 + 512, :], (1, 4)) + (lc[h] - log_total[0:1, :])
            hinge = 0.5 + 0.5 * jnp.tanh(0.5 * t)
            for e in range(2):
                part = slice(e * 256, e * 256 + 256)
                grad = t[part] * a[e][g, h] - b[e][g, h] + n[e][g, h].astype(F32) * hinge[part]
                grads[h, g * 512 + e * 256 : g * 512 + e * 256 + 256, :] = grad.astype(BF16)

    @pl.when(role == W_ROLE)
    def _():
        col_grad(w, c, grads, send)

    @pl.when(role != W_ROLE)
    def _():
        row_grad(w, c, grads, send)


def row_grad(w, c, grads, out):
    for g in range(2):
        total = jnp.zeros((512, 512), F32)
        for h in range(2):
            ch = c[:, h * 64 : h * 64 + 64, :].reshape(512, 512)
            total += lax.dot_general(grads[h, g * 512 : g * 512 + 512, :], ch, NT, preferred_element_type=F32)
        out[4 * g : 4 * g + 4] = total.reshape(4, 128, 512).astype(out.dtype)


def col_grad(w, c, grads, out):
    w_all = w[...].reshape(1024, 512)
    for h in range(2):
        total = lax.dot_general(w_all, grads[h], TN, preferred_element_type=F32)
        out[:, h * 64 : h * 64 + 64, :] = total.reshape(8, 64, 512).astype(out.dtype)


def front(here, gathered, factors, lr, lc, log_total):
    first = log_total is None
    args = [here, *gathered, *factors, lr, lc] + ([] if first else [log_total])
    shape = (8, 128, 512)
    out_shape = [pltpu.VMEM(s, BF16) for s in (shape, shape, (2, 1024, 512), shape)]
    if first:
        out_shape.append(pltpu.VMEM((8, 512), F32))
    return vmem_kernel(
        functools.partial(front_kernel, first),
        16,
        in_specs=[IN_SMEM] + [IN_VMEM] * (len(args) - 1),
        out_specs=[IN_VMEM] * len(out_shape),
        out_shape=out_shape,
        cost_estimate=pl.CostEstimate(flops=3 * 10**9, bytes_accessed=16 * 2**20, transcendentals=2**20),
        name="cell_grads",
    )(*args)


def back_kernel(here, w, c, grads, keep):
    role, _, _ = place(here)

    @pl.when(role == W_ROLE)
    def _():
        row_grad(w, c, grads, keep)

    @pl.when(role != W_ROLE)
    def _():
        col_grad(w, c, grads, keep)


def back(here, w, c, grads):
    return vmem_kernel(
        back_kernel,
        12,
        in_specs=[IN_SMEM] + [IN_VMEM] * 3,
        out_specs=IN_VMEM,
        out_shape=pltpu.VMEM(w.shape, F32),
        cost_estimate=pl.CostEstimate(flops=10**9, bytes_accessed=8 * 2**20, transcendentals=0),
        name="own_products",
    )(here, w, c, grads)


def merge_kernel(here, keep, extra, *outs):
    at, _ = own_place(here)
    for k, out in enumerate(outs):
        block = pl.ds(2 * ((at + k) & 3), 2)
        out[...] = (keep[block] + extra[block].astype(F32)).astype(BF16)


def merge(here, keep, extra):
    return vmem_kernel(
        merge_kernel,
        8,
        in_specs=[IN_SMEM] + [IN_VMEM] * 2,
        out_specs=[IN_VMEM] * 4,
        out_shape=[pltpu.VMEM((2, 128, 512), BF16)] * 4,
        name="core_sum",
    )(here, keep, extra)


def ring_sum_kernel(here, *refs):
    *terms, mine, theirs = refs
    _, side = own_place(here)

    def total(s):
        out = terms[0][s].astype(F32)
        for term in terms[1:4]:
            out += term[s].astype(F32)
        return out

    mine[...] = total(side)
    theirs[...] = total(1 - side).astype(BF16)


def ring_sum(here, terms, *after):
    return vmem_kernel(
        ring_sum_kernel,
        8,
        in_specs=[IN_SMEM] + [IN_VMEM] * (4 + len(after)),
        out_specs=[IN_VMEM] * 2,
        out_shape=[pltpu.VMEM((128, 512), F32), pltpu.VMEM((128, 512), BF16)],
        name="ring_sum",
    )(here, *terms, *after)


def pack_kernel(here, *refs):
    at, _ = own_place(here)
    for k in range(4):
        refs[-1][(at - k) & 3] = refs[k][...]


def pack(here, shards, *after):
    return vmem_kernel(
        pack_kernel,
        4,
        in_specs=[IN_SMEM] + [IN_VMEM] * (4 + len(after)),
        out_specs=IN_VMEM,
        out_shape=pltpu.VMEM((4, *shards[0].shape), BF16),
        name="in_ring_order",
    )(here, *shards, *after)


def update_kernel(mine, theirs, embed, new, payload=None):
    fresh = embed[...] - RATE * (mine[...] + theirs[...].astype(F32))
    new[...] = fresh
    if payload is not None:
        payload[...] = fresh.astype(BF16)


def update(mine, theirs, embed, last):
    more = not last
    return vmem_kernel(
        update_kernel,
        4,
        in_specs=[IN_VMEM] * 3,
        out_specs=[IN_VMEM] * (1 + more),
        out_shape=[pltpu.VMEM(embed.shape, F32)] + [pltpu.VMEM(embed.shape, BF16)] * more,
        name="update",
    )(mine, theirs, embed)


def logs_kernel(row_marginals, col_marginals, lr, lc, rows, cols, sem):
    copies = [
        pltpu.make_async_copy(row_marginals, rows, sem.at[0]),
        pltpu.make_async_copy(col_marginals, cols, sem.at[1]),
    ]
    for copy in copies:
        copy.start()
    for copy in copies:
        copy.wait()
    log_rows = jnp.log(rows[...].astype(F32))
    log_cols = jnp.log(cols[...].astype(F32))
    for k in range(8):
        lr[k * 128 : k * 128 + 128, :] = jnp.broadcast_to(log_rows[k : k + 1, :], (128, 128)).T
    for h in range(2):
        lc[h] = jnp.concatenate([log_cols[4 * h + k : 4 * h + k + 1, :] for k in range(4)], axis=1)


def logs(row_marginals, col_marginals):
    return vmem_kernel(
        logs_kernel,
        4,
        in_specs=[IN_HBM] * 2,
        out_specs=[IN_VMEM] * 2,
        out_shape=[pltpu.VMEM((1024, 128), F32), pltpu.VMEM((2, 1, 512), F32)],
        scratch_shapes=[pltpu.VMEM((8, 128), jnp.int32)] * 2 + [pltpu.SemaphoreType.DMA((2,))],
        name="log_marginals",
    )(row_marginals.reshape(8, 128), col_marginals.reshape(8, 128))


def prep_kernel(here, row_embed, col_embed, marginals, embed, payload, sums, sem):
    sum_copy = pltpu.make_async_copy(marginals, sums, sem.at[0])
    sum_copy.start()

    @pl.when(place(here)[0] == W_ROLE)
    def _():
        copy = pltpu.make_async_copy(row_embed, embed, sem.at[1])
        copy.start()
        copy.wait()

    @pl.when(place(here)[0] != W_ROLE)
    def _():
        low = pltpu.make_async_copy(col_embed.at[:, pl.ds(0, 512)], embed.at[pl.ds(0, 64)], sem.at[1])
        high = pltpu.make_async_copy(col_embed.at[:, pl.ds(512, 512)], embed.at[pl.ds(64, 64)], sem.at[2])
        low.start()
        high.start()
        low.wait()
        high.wait()

    sum_copy.wait()
    mine = embed[...].astype(BF16)
    rest = jnp.sum(sums[...].astype(F32), axis=(0, 1), keepdims=True)
    line = lax.broadcasted_iota(jnp.int32, (8, 512), 0)
    extra = jnp.zeros((8, 512), F32)
    for k in range(3):
        piece = rest.astype(BF16).astype(F32)
        extra = jnp.where(line == k, piece, extra)
        rest = rest - piece
    payload[:128, :] = mine
    payload[128:, :] = extra.astype(BF16)


def prep(here, row_embed, col_embed, marginals):
    return vmem_kernel(
        prep_kernel,
        4,
        in_specs=[IN_SMEM, IN_HBM, IN_HBM, IN_HBM],
        out_specs=[IN_VMEM] * 2,
        out_shape=[pltpu.VMEM((128, 512), F32), pltpu.VMEM((136, 512), BF16)],
        scratch_shapes=[pltpu.VMEM((8, 128), jnp.int32), pltpu.SemaphoreType.DMA((3,))],
        name="first_payload",
    )(here, row_embed, col_embed, marginals.reshape(8, 128))


def finish_kernel(here, embed, theirs, new_row, new_col, sem):
    def write(row, col):
        copies = [
            pltpu.make_async_copy(row, new_row, sem.at[0]),
            pltpu.make_async_copy(col.at[pl.ds(0, 64)], new_col.at[:, pl.ds(0, 512)], sem.at[1]),
            pltpu.make_async_copy(col.at[pl.ds(64, 64)], new_col.at[:, pl.ds(512, 512)], sem.at[2]),
        ]
        for copy in copies:
            copy.start()
        for copy in copies:
            copy.wait()

    @pl.when(place(here)[0] == W_ROLE)
    def _():
        write(embed, theirs)

    @pl.when(place(here)[0] != W_ROLE)
    def _():
        write(theirs, embed)


def finish(here, embed, theirs):
    return vmem_kernel(
        finish_kernel,
        4,
        in_specs=[IN_SMEM, IN_VMEM, IN_VMEM],
        out_specs=[IN_HBM] * 2,
        out_shape=[pltpu.HBM((128, 512), F32), pltpu.HBM((64, 1024), F32)],
        scratch_shapes=[pltpu.SemaphoreType.DMA((3,))],
        name="results",
    )(here, embed, theirs)


def per_device(swap, across, along, row_embed, col_embed, counts, block_rows, block_cols, row_marginals, col_marginals):
    here = lax.axis_index(AXES).astype(jnp.int32).reshape(1)
    steps = counts.shape[0]

    def other_core(x):
        return lax.ppermute(x, "rep", swap)

    def other_side(x):
        return lax.ppermute(x, AXES, across)

    def ring(x, k):
        return lax.ppermute(x, AXES, along[k])

    embed, payload = prep(here, row_embed, col_embed, row_marginals)
    payload, block_rows, block_cols, row_marginals, col_marginals = lax.optimization_barrier(
        (payload, block_rows, block_cols, row_marginals, col_marginals)
    )
    lr, lc = logs(row_marginals, col_marginals)
    rows = block_rows.reshape(block_rows.shape[:2])
    cols = block_cols.reshape(block_cols.shape[:2])

    low, done_low = abn(counts, rows, cols, 0, 0)
    log_total = None
    for step in range(steps):
        last = step + 1 == steps
        payload, rows, cols = lax.optimization_barrier((payload, rows, cols))
        far = other_side(payload)
        near = [payload] + [ring(payload, k) for k in (1, 3, 2)]
        far = [far] + [ring(far, k) for k in (1, 3, 2)]
        high, done_high = abn(counts, rows, cols, step, 1)
        in_order = lambda x: [x[0], x[1], x[3], x[2]]
        near = pack(here, in_order(near), done_low)
        near_other = other_core(near)
        far = pack(here, in_order(far), done_high)
        far_other = other_core(far)
        res = front(here, (near, far, near_other, far_other), low + high, lr, lc, log_total)
        if step == 0:
            *res, log_total = res
        w, c, grads, send = res
        extra = other_core(send)
        keep = back(here, w, c, grads)
        terms = merge(here, keep, extra)
        after = []
        if not last:
            *terms, rows, cols = lax.optimization_barrier((*terms, rows, cols))
            low, done_low = abn(counts, rows, cols, step + 1, 0)
            after = [done_low]
        got = {k: ring(terms[k], k) for k in (2, 1, 3)}
        mine, theirs = ring_sum(here, [terms[0], got[1], got[2], got[3]], *after)
        res = update(mine, other_side(theirs), embed, last)
        if last:
            (embed,) = res
        else:
            embed, payload = res
    return tuple(finish(here, embed, other_core(embed)))


def solution(mesh):
    n_row, n_col = mesh.shape["row"], mesh.shape["col"]
    across, along = [], {1: [], 2: [], 3: []}
    for r in range(n_row):
        for c in range(n_col):
            for p in range(2):
                i = (r * n_col + c) * 2 + p
                if p == W_ROLE:
                    across.append((i, (r * n_col + (c ^ 1)) * 2 + p))
                    for k in along:
                        along[k].append((i, (r * n_col + (c + 2 * k) % n_col) * 2 + p))
                else:
                    across.append((i, ((r ^ 1) * n_col + c) * 2 + p))
                    for k in along:
                        along[k].append((i, ((r + 2 * k) % n_row * n_col + c) * 2 + p))
    swap = [(0, 1), (1, 0)]
    return jax.shard_map(
        functools.partial(per_device, swap, across, along),
        mesh=mesh,
        in_specs=(
            P(("row", "col"), None),
            P("row", "col"),
            P(None, "rep", "row", "col"),
            P(None, "rep", "row", "col"),
            P(None, "rep", "row", "col"),
            P("row"),
            P("col"),
        ),
        out_specs=(P(("row", "col"), None), P("row", "col")),
        check_vma=False,
    )
```

```python
import functools

import jax
import jax.numpy as jnp
from jax import lax
from jax.experimental import pallas as pl
from jax.experimental.pallas import tpu as pltpu
from jax.sharding import PartitionSpec as P

RATE = 0.002
AXES = ("row", "col", "rep")
F32 = jnp.float32
BF16 = jnp.bfloat16
W_ROLE = 1
PIECE = 32
STRIP = 16
NT = (((1,), (1,)), ((), ()))
TN = (((0,), (0,)), ((), ()))
IN_VMEM = pl.BlockSpec(memory_space=pltpu.VMEM)
IN_HBM = pl.BlockSpec(memory_space=pltpu.HBM)
IN_SMEM = pl.BlockSpec(memory_space=pltpu.SMEM)


def vmem_kernel(kernel, mib, **kwargs):
    call = pl.pallas_call(kernel, compiler_params=pltpu.CompilerParams(vmem_limit_bytes=mib * 2**20), **kwargs)

    def run(*args):
        spaces = {id(IN_VMEM): pltpu.VMEM, id(IN_HBM): pltpu.HBM}
        return call(
            *(
                pltpu.with_memory_space_constraint(x, spaces[id(spec)]) if id(spec) in spaces else x
                for x, spec in zip(args, kwargs["in_specs"])
            )
        )

    return run


def place(here):
    i = here[0]
    col, row = (i >> 1) & 7, i >> 4
    return i & 1, (col >> 1, col & 1), (row >> 1, row & 1)


def own_place(here):
    role, of_w, of_c = place(here)
    return [jnp.where(role == W_ROLE, p, q) for p, q in zip(of_w, of_c)]


def abn_kernel(step, half, rows_in, cols_in, counts, after, a, b, n, done, rows, cols, held, seen, sem):
    slots, extent = counts.shape[1], counts.shape[2] // 2

    def piece(i):
        part = pl.ds(half * extent + i * PIECE, PIECE)
        return pltpu.make_async_copy(counts.at[step, :, part, :], held.at[i], sem.at[i])

    pieces = extent // PIECE
    indices = [
        pltpu.make_async_copy(rows_in.at[step], rows, sem.at[pieces]),
        pltpu.make_async_copy(cols_in.at[step], cols, sem.at[pieces + 1]),
    ]
    for copy in indices:
        copy.start()
    for i in range(pieces):
        piece(i).start()
    for ref in (a, b, done, seen):
        ref[...] = jnp.zeros(ref.shape, F32)
    for copy in indices:
        copy.wait()
    sampled = {}
    for g in range(2):
        for h in range(2):
            total = jnp.int32(0)
            for slot in range(slots):
                total += ((rows[0, slot] == g) & (cols[0, slot] == h)).astype(jnp.int32)
            sampled[g, h] = total.astype(F32)
    for i in range(extent // PIECE):
        piece(i).wait()

        def strip(j, carry):
            here = pl.ds(pl.multiple_of(j * STRIP, STRIP), STRIP)
            part = pl.ds(pl.multiple_of(i * PIECE + j * STRIP, STRIP), STRIP)
            for slot in range(slots):
                xf = held[i, slot, here, :].astype(F32)
                top = jnp.maximum(xf, 1.0)
                root = xf * lax.rsqrt(top)
                at = (rows[0, slot], cols[0, slot], part, slice(None))
                a[at] += root
                b[at] += (0.1 + 0.25 * root) * jnp.log(top)
                seen[at] += jnp.minimum(xf, 1.0)
            for g in range(2):
                for h in range(2):
                    number = seen[g, h, part, :]
                    a[g, h, part, :] = 0.1 * number + 0.25 * a[g, h, part, :]
                    n[g, h, part, :] = (sampled[g, h] - number).astype(BF16)
            return carry

        lax.fori_loop(0, PIECE // STRIP, strip, 0)


def abn(counts, rows, cols, step, half, after):
    slots, block = counts.shape[1], counts.shape[2]
    shape = (2, 2, block // 2, block)
    pieces = block // 2 // PIECE
    *factors, done = vmem_kernel(
        functools.partial(abn_kernel, step, half),
        8,
        in_specs=[IN_HBM, IN_HBM, IN_HBM, IN_VMEM],
        out_specs=[IN_VMEM] * 4,
        out_shape=[pltpu.VMEM(shape, d) for d in (F32, F32, BF16)] + [pltpu.VMEM((8, 128), F32)],
        scratch_shapes=[
            pltpu.SMEM((1, slots), jnp.int32),
            pltpu.SMEM((1, slots), jnp.int32),
            pltpu.VMEM((pieces, slots, PIECE, block), jnp.int32),
            pltpu.VMEM(shape, F32),
            pltpu.SemaphoreType.DMA((pieces + 2,)),
        ],
        cost_estimate=pl.CostEstimate(flops=3 * 10**9, bytes_accessed=4 * 2**20, transcendentals=2 * 2**20),
        name="count_factors",
    )(rows, cols, counts, after)
    return factors, done


def front_kernel(first, here, done, *refs):
    own, other, refs = refs[:4], refs[4:8], refs[8:]
    a, b, n = refs[0:6:3], refs[1:6:3], refs[2:6:3]
    lr, lc, *refs = refs[6:]
    if first:
        w, c, grads, send, log_total = refs
    else:
        log_total, w, c, grads, send = refs
    role, (w_at, _), (c_at, _) = place(here)

    def assemble(of_w, of_c):
        for k in range(4):
            w[pl.ds(2 * ((w_at - k) & 3), 2)] = of_w[k][:, :128, :]
            c[pl.ds(2 * ((c_at - k) & 3), 2)] = of_c[k][:, :128, :]
        if first:
            pieces = jnp.zeros((8, 512), F32)
            for k in range(4):
                pieces += jnp.sum(of_c[k][:, 128:, :].astype(F32), axis=0)
            log_total[...] = jnp.broadcast_to(jnp.log(jnp.sum(pieces, axis=0, keepdims=True)), log_total.shape)

    @pl.when(role == W_ROLE)
    def _():
        assemble(own, other)

    @pl.when(role != W_ROLE)
    def _():
        assemble(other, own)

    for g in range(2):
        wg = w[4 * g : 4 * g + 4].reshape(512, 512)
        for h in range(2):
            ch = c[:, h * 64 : h * 64 + 64, :].reshape(512, 512)
            dots = jnp.dot(wg, ch, preferred_element_type=F32)
            t = dots + jnp.tile(lr[g * 512 : g * 512 + 512, :], (1, 4)) + (lc[h] - log_total[0:1, :])
            hinge = 0.5 + 0.5 * jnp.tanh(0.5 * t)
            for e in range(2):
                part = slice(e * 256, e * 256 + 256)
                grad = t[part] * a[e][g, h] - b[e][g, h] + n[e][g, h].astype(F32) * hinge[part]
                grads[h, g * 512 + e * 256 : g * 512 + e * 256 + 256, :] = grad.astype(BF16)

    @pl.when(role == W_ROLE)
    def _():
        col_grad(w, c, grads, send)

    @pl.when(role != W_ROLE)
    def _():
        row_grad(w, c, grads, send)


def row_grad(w, c, grads, out):
    for g in range(2):
        total = jnp.zeros((512, 512), F32)
        for h in range(2):
            ch = c[:, h * 64 : h * 64 + 64, :].reshape(512, 512)
            total += lax.dot_general(grads[h, g * 512 : g * 512 + 512, :], ch, NT, preferred_element_type=F32)
        out[4 * g : 4 * g + 4] = total.reshape(4, 128, 512).astype(out.dtype)


def col_grad(w, c, grads, out):
    w_all = w[...].reshape(1024, 512)
    for h in range(2):
        total = lax.dot_general(w_all, grads[h], TN, preferred_element_type=F32)
        out[:, h * 64 : h * 64 + 64, :] = total.reshape(8, 64, 512).astype(out.dtype)


def front(here, done, gathered, factors, lr, lc, log_total):
    first = log_total is None
    args = [here, done, *gathered, *factors, lr, lc] + ([] if first else [log_total])
    shape = (8, 128, 512)
    out_shape = [pltpu.VMEM(s, BF16) for s in (shape, shape, (2, 1024, 512), shape)]
    if first:
        out_shape.append(pltpu.VMEM((8, 512), F32))
    return vmem_kernel(
        functools.partial(front_kernel, first),
        16,
        in_specs=[IN_SMEM] + [IN_VMEM] * (len(args) - 1),
        out_specs=[IN_VMEM] * len(out_shape),
        out_shape=out_shape,
        cost_estimate=pl.CostEstimate(flops=3 * 10**9, bytes_accessed=16 * 2**20, transcendentals=2**20),
        name="cell_grads",
    )(*args)


def back_kernel(here, w, c, grads, keep):
    role, _, _ = place(here)

    @pl.when(role == W_ROLE)
    def _():
        row_grad(w, c, grads, keep)

    @pl.when(role != W_ROLE)
    def _():
        col_grad(w, c, grads, keep)


def back(here, w, c, grads):
    return vmem_kernel(
        back_kernel,
        12,
        in_specs=[IN_SMEM] + [IN_VMEM] * 3,
        out_specs=IN_VMEM,
        out_shape=pltpu.VMEM(w.shape, F32),
        cost_estimate=pl.CostEstimate(flops=10**9, bytes_accessed=8 * 2**20, transcendentals=0),
        name="own_products",
    )(here, w, c, grads)


def merge_kernel(here, keep, extra, *outs):
    at, _ = own_place(here)
    for k, out in enumerate(outs):
        block = pl.ds(2 * ((at + k) & 3), 2)
        out[...] = (keep[block] + extra[block].astype(F32)).astype(BF16)


def merge(here, keep, extra):
    return vmem_kernel(
        merge_kernel,
        8,
        in_specs=[IN_SMEM] + [IN_VMEM] * 2,
        out_specs=[IN_VMEM] * 4,
        out_shape=[pltpu.VMEM((2, 128, 512), BF16)] * 4,
        name="core_sum",
    )(here, keep, extra)


def ring_sum_kernel(last, here, *refs):
    terms, outs = refs[:4], refs[-2:]
    _, side = own_place(here)

    def total(s):
        out = terms[0][s].astype(F32)
        for term in terms[1:4]:
            out += term[s].astype(F32)
        return out

    mine, theirs = outs
    if last:
        mine[...] = total(side)
        theirs[...] = total(1 - side).astype(BF16)
    else:
        for s in range(2):
            mine[s] = total(s)
            theirs[s] = mine[s].astype(BF16)


def ring_sum(here, terms, last, *after):
    shape = (128, 512) if last else (2, 128, 512)
    return vmem_kernel(
        functools.partial(ring_sum_kernel, last),
        8,
        in_specs=[IN_SMEM] + [IN_VMEM] * (4 + len(after)),
        out_specs=[IN_VMEM] * 2,
        out_shape=[pltpu.VMEM(shape, F32), pltpu.VMEM(shape, BF16)],
        name="ring_sum",
    )(here, *terms, *after)


def pair_kernel(here, mine, far, done, out):
    _, side = own_place(here)
    out[side] = mine[...]
    out[1 - side] = far[...]


def pair(here, mine, far, done):
    return vmem_kernel(
        pair_kernel,
        4,
        in_specs=[IN_SMEM] + [IN_VMEM] * 3,
        out_specs=IN_VMEM,
        out_shape=pltpu.VMEM((2, *mine.shape), BF16),
        name="both_sides",
    )(here, mine, far, done)


def update_kernel(mine, theirs, embed, new):
    new[...] = embed[...] - RATE * (mine[...] + theirs[...].astype(F32))


def update(mine, theirs, embed):
    return vmem_kernel(
        update_kernel,
        4,
        in_specs=[IN_VMEM] * 3,
        out_specs=IN_VMEM,
        out_shape=pltpu.VMEM(embed.shape, F32),
        name="update",
    )(mine, theirs, embed)


def update_both_kernel(here, mine, theirs, embed, far, done, new, payload):
    _, side = own_place(here)

    def fresh(s, old):
        return old[...] - RATE * (mine[s] + theirs[s].astype(F32))

    new[...] = fresh(side, embed)
    payload[side] = new[...].astype(BF16)
    payload[1 - side] = fresh(1 - side, far).astype(BF16)


def update_both(here, mine, theirs, embed, far, done):
    return vmem_kernel(
        update_both_kernel,
        8,
        in_specs=[IN_SMEM] + [IN_VMEM] * 5,
        out_specs=[IN_VMEM] * 2,
        out_shape=[pltpu.VMEM(embed.shape, F32), pltpu.VMEM(mine.shape, BF16)],
        name="update",
    )(here, mine, theirs, embed, far, done)


def prep_kernel(here, row_embed, col_embed, row_marginals, col_marginals, embed, payload, lr, lc, rows, cols, sem):
    row_copy = pltpu.make_async_copy(row_marginals, rows, sem.at[0])
    col_copy = pltpu.make_async_copy(col_marginals, cols, sem.at[3])
    row_copy.start()
    col_copy.start()

    @pl.when(place(here)[0] == W_ROLE)
    def _():
        copy = pltpu.make_async_copy(row_embed, embed, sem.at[1])
        copy.start()
        copy.wait()

    @pl.when(place(here)[0] != W_ROLE)
    def _():
        low = pltpu.make_async_copy(col_embed.at[:, pl.ds(0, 512)], embed.at[pl.ds(0, 64)], sem.at[1])
        high = pltpu.make_async_copy(col_embed.at[:, pl.ds(512, 512)], embed.at[pl.ds(64, 64)], sem.at[2])
        low.start()
        high.start()
        low.wait()
        high.wait()

    row_copy.wait()
    col_copy.wait()
    mine = embed[...].astype(BF16)
    row_values = rows[...].astype(F32)
    rest = jnp.sum(row_values, axis=(0, 1), keepdims=True)
    line = lax.broadcasted_iota(jnp.int32, (8, 512), 0)
    extra = jnp.zeros((8, 512), F32)
    for k in range(3):
        piece = rest.astype(BF16).astype(F32)
        extra = jnp.where(line == k, piece, extra)
        rest = rest - piece
    payload[:128, :] = mine
    payload[128:, :] = extra.astype(BF16)
    log_rows = jnp.log(row_values)
    log_cols = jnp.log(cols[...].astype(F32))
    for k in range(8):
        lr[k * 128 : k * 128 + 128, :] = jnp.broadcast_to(log_rows[k : k + 1, :], (128, 128)).T
    for h in range(2):
        lc[h] = jnp.concatenate([log_cols[4 * h + k : 4 * h + k + 1, :] for k in range(4)], axis=1)


def prep(here, row_embed, col_embed, row_marginals, col_marginals):
    return vmem_kernel(
        prep_kernel,
        4,
        in_specs=[IN_SMEM] + [IN_HBM] * 4,
        out_specs=[IN_VMEM] * 4,
        out_shape=[
            pltpu.VMEM((128, 512), F32),
            pltpu.VMEM((136, 512), BF16),
            pltpu.VMEM((1024, 128), F32),
            pltpu.VMEM((2, 1, 512), F32),
        ],
        scratch_shapes=[pltpu.VMEM((8, 128), jnp.int32)] * 2 + [pltpu.SemaphoreType.DMA((4,))],
        name="first_payload",
    )(here, row_embed, col_embed, row_marginals.reshape(8, 128), col_marginals.reshape(8, 128))


def finish_kernel(here, embed, theirs, new_row, new_col, sem):
    def write(row, col):
        copies = [
            pltpu.make_async_copy(row, new_row, sem.at[0]),
            pltpu.make_async_copy(col.at[pl.ds(0, 64)], new_col.at[:, pl.ds(0, 512)], sem.at[1]),
            pltpu.make_async_copy(col.at[pl.ds(64, 64)], new_col.at[:, pl.ds(512, 512)], sem.at[2]),
        ]
        for copy in copies:
            copy.start()
        for copy in copies:
            copy.wait()

    @pl.when(place(here)[0] == W_ROLE)
    def _():
        write(embed, theirs)

    @pl.when(place(here)[0] != W_ROLE)
    def _():
        write(theirs, embed)


def finish(here, embed, theirs):
    return vmem_kernel(
        finish_kernel,
        4,
        in_specs=[IN_SMEM, IN_VMEM, IN_VMEM],
        out_specs=[IN_HBM] * 2,
        out_shape=[pltpu.HBM((128, 512), F32), pltpu.HBM((64, 1024), F32)],
        scratch_shapes=[pltpu.SemaphoreType.DMA((3,))],
        name="results",
    )(here, embed, theirs)


def per_device(swap, across, along, row_embed, col_embed, counts, block_rows, block_cols, row_marginals, col_marginals):
    here = lax.axis_index(AXES).astype(jnp.int32).reshape(1)
    steps = counts.shape[0]

    def other_core(x):
        return lax.ppermute(x, "rep", swap)

    def other_side(x):
        return lax.ppermute(x, AXES, across)

    def ring(x, k):
        return lax.ppermute(x, AXES, along[k])

    embed, payload, lr, lc = prep(here, row_embed, col_embed, row_marginals, col_marginals)
    rows = block_rows.reshape(steps, 1, -1)
    cols = block_cols.reshape(steps, 1, -1)

    low, done = abn(counts, rows, cols, 0, 0, payload)
    payload = pair(here, payload, other_side(payload), done)
    log_total = None
    for step in range(steps):
        last = step + 1 == steps
        got = {k: ring(payload, k) for k in (2, 1, 3)}
        if step == 0:
            high, done = abn(counts, rows, cols, 0, 1, payload)
            got[3], done = lax.optimization_barrier((got[3], done))
        own = [payload, got[1], got[2], got[3]]
        other = [other_core(x) for x in own]
        res = front(here, done, own + other, low + high, lr, lc, log_total)
        if step == 0:
            *res, log_total = res
        w, c, grads, send = res
        extra = other_core(send)
        keep = back(here, w, c, grads)
        terms = merge(here, keep, extra)
        if not last:
            embed, *terms = lax.optimization_barrier((embed, *terms))
        got = {k: ring(terms[k], k) for k in (2, 1, 3)}
        terms = [terms[0], got[1], got[2], got[3]]
        if last:
            mine, theirs = ring_sum(here, terms, last)
            embed = update(mine, other_side(theirs), embed)
        else:
            far = other_side(embed)
            low, done = abn(counts, rows, cols, step + 1, 0, terms[0])
            mine, theirs = ring_sum(here, terms, last, done)
            high, done = abn(counts, rows, cols, step + 1, 1, theirs)
            embed, payload = update_both(here, mine, other_side(theirs), embed, far, done)
    return tuple(finish(here, embed, other_core(embed)))


def solution(mesh):
    n_row, n_col = mesh.shape["row"], mesh.shape["col"]
    across, along = [], {1: [], 2: [], 3: []}
    for r in range(n_row):
        for c in range(n_col):
            for p in range(2):
                i = (r * n_col + c) * 2 + p
                if p == W_ROLE:
                    across.append((i, (r * n_col + (c ^ 1)) * 2 + p))
                    for k in along:
                        along[k].append((i, (r * n_col + (c + 2 * k) % n_col) * 2 + p))
                else:
                    across.append((i, ((r ^ 1) * n_col + c) * 2 + p))
                    for k in along:
                        along[k].append((i, ((r + 2 * k) % n_row * n_col + c) * 2 + p))
    swap = [(0, 1), (1, 0)]
    return jax.shard_map(
        functools.partial(per_device, swap, across, along),
        mesh=mesh,
        in_specs=(
            P(("row", "col"), None),
            P("row", "col"),
            P(None, "rep", "row", "col"),
            P(None, "rep", "row", "col"),
            P(None, "rep", "row", "col"),
            P("row"),
            P("col"),
        ),
        out_specs=(P(("row", "col"), None), P("row", "col")),
        check_vma=False,
    )
```

```python
import functools

import jax
import jax.numpy as jnp
from jax import lax
from jax.experimental import pallas as pl
from jax.experimental.pallas import tpu as pltpu
from jax.sharding import PartitionSpec as P

RATE = 0.002
AXES = ("row", "col", "rep")
F32 = jnp.float32
BF16 = jnp.bfloat16
W_ROLE = 1
PIECE = 32
STRIP = 16
NT = (((1,), (1,)), ((), ()))
TN = (((0,), (0,)), ((), ()))
IN_VMEM = pl.BlockSpec(memory_space=pltpu.VMEM)
IN_HBM = pl.BlockSpec(memory_space=pltpu.HBM)
IN_SMEM = pl.BlockSpec(memory_space=pltpu.SMEM)


def vmem_kernel(kernel, mib, **kwargs):
    call = pl.pallas_call(kernel, compiler_params=pltpu.CompilerParams(vmem_limit_bytes=mib * 2**20), **kwargs)

    def run(*args):
        spaces = {id(IN_VMEM): pltpu.VMEM, id(IN_HBM): pltpu.HBM}
        return call(
            *(
                pltpu.with_memory_space_constraint(x, spaces[id(spec)]) if id(spec) in spaces else x
                for x, spec in zip(args, kwargs["in_specs"])
            )
        )

    return run


def place(here):
    i = here[0]
    col, row = (i >> 1) & 7, i >> 4
    return i & 1, (col >> 1, col & 1), (row >> 1, row & 1)


def own_place(here):
    role, of_w, of_c = place(here)
    return [jnp.where(role == W_ROLE, p, q) for p, q in zip(of_w, of_c)]


def abn_kernel(step, half, rows_in, cols_in, counts, after, a, b, n, done, rows, cols, held, seen, sem):
    slots, extent = counts.shape[1], counts.shape[2] // 2

    def piece(i):
        part = pl.ds(half * extent + i * PIECE, PIECE)
        return pltpu.make_async_copy(counts.at[step, :, part, :], held.at[i], sem.at[i])

    pieces = extent // PIECE
    indices = [
        pltpu.make_async_copy(rows_in.at[step], rows, sem.at[pieces]),
        pltpu.make_async_copy(cols_in.at[step], cols, sem.at[pieces + 1]),
    ]
    for copy in indices:
        copy.start()
    for i in range(pieces):
        piece(i).start()
    for ref in (a, b, done, seen):
        ref[...] = jnp.zeros(ref.shape, F32)
    for copy in indices:
        copy.wait()
    sampled = {}
    for g in range(2):
        for h in range(2):
            total = jnp.int32(0)
            for slot in range(slots):
                total += ((rows[0, slot] == g) & (cols[0, slot] == h)).astype(jnp.int32)
            sampled[g, h] = total.astype(F32)
    for i in range(extent // PIECE):
        piece(i).wait()

        def strip(j, carry):
            here = pl.ds(pl.multiple_of(j * STRIP, STRIP), STRIP)
            part = pl.ds(pl.multiple_of(i * PIECE + j * STRIP, STRIP), STRIP)
            for slot in range(slots):
                xf = held[i, slot, here, :].astype(F32)
                top = jnp.maximum(xf, 1.0)
                root = xf * lax.rsqrt(top)
                at = (rows[0, slot], cols[0, slot], part, slice(None))
                a[at] += root
                b[at] += (0.1 + 0.25 * root) * jnp.log(top)
                seen[at] += jnp.minimum(xf, 1.0)
            for g in range(2):
                for h in range(2):
                    number = seen[g, h, part, :]
                    zeros = 0.5 * (sampled[g, h] - number)
                    a[g, h, part, :] = 0.1 * number + 0.25 * a[g, h, part, :]
                    b[g, h, part, :] -= zeros
                    n[g, h, part, :] = zeros.astype(BF16)
            return carry

        lax.fori_loop(0, PIECE // STRIP, strip, 0)


def abn(counts, rows, cols, step, half, after):
    slots, block = counts.shape[1], counts.shape[2]
    shape = (2, 2, block // 2, block)
    pieces = block // 2 // PIECE
    *factors, done = vmem_kernel(
        functools.partial(abn_kernel, step, half),
        8,
        in_specs=[IN_HBM, IN_HBM, IN_HBM, IN_VMEM],
        out_specs=[IN_VMEM] * 4,
        out_shape=[pltpu.VMEM(shape, d) for d in (F32, F32, BF16)] + [pltpu.VMEM((8, 128), F32)],
        scratch_shapes=[
            pltpu.SMEM((1, slots), jnp.int32),
            pltpu.SMEM((1, slots), jnp.int32),
            pltpu.VMEM((pieces, slots, PIECE, block), jnp.int32),
            pltpu.VMEM(shape, F32),
            pltpu.SemaphoreType.DMA((pieces + 2,)),
        ],
        cost_estimate=pl.CostEstimate(flops=3 * 10**9, bytes_accessed=4 * 2**20, transcendentals=2 * 2**20),
        name="count_factors",
    )(rows, cols, counts, after)
    return factors, done


def front_kernel(first, here, done, *refs):
    own, other, refs = refs[:4], refs[4:8], refs[8:]
    a, b, n = refs[0:6:3], refs[1:6:3], refs[2:6:3]
    lr, lc, *refs = refs[6:]
    if first:
        w, c, grads, send, log_total = refs
    else:
        log_total, w, c, grads, send = refs
    role, (w_at, _), (c_at, _) = place(here)

    def assemble(of_w, of_c):
        for k in range(4):
            w[pl.ds(2 * ((w_at - k) & 3), 2)] = of_w[k][:, :128, :]
            c[pl.ds(2 * ((c_at - k) & 3), 2)] = of_c[k][:, :128, :]
        if first:
            pieces = jnp.zeros((8, 512), F32)
            for k in range(4):
                pieces += jnp.sum(of_c[k][:, 128:, :].astype(F32), axis=0)
            log_total[...] = jnp.broadcast_to(jnp.log(jnp.sum(pieces, axis=0, keepdims=True)), log_total.shape)

    def body(of_w, of_c, send_rows):
        assemble(of_w, of_c)
        held = {}
        for g in range(2):
            wg = w[4 * g : 4 * g + 4].reshape(512, 512)
            for h in range(2):
                ch = c[:, h * 64 : h * 64 + 64, :].reshape(512, 512)
                dots = jnp.dot(wg, ch, preferred_element_type=F32)
                t = dots + jnp.tile(lr[g * 512 : g * 512 + 512, :], (1, 4)) + (lc[h] - log_total[0:1, :])
                hinge = jnp.tanh(0.5 * t)
                parts = []
                for e in range(2):
                    part = slice(e * 256, e * 256 + 256)
                    grad = t[part] * a[e][g, h] - b[e][g, h] + n[e][g, h].astype(F32) * hinge[part]
                    parts.append(grad.astype(BF16))
                grad = jnp.concatenate(parts, axis=0)
                grads[h, g * 512 : g * 512 + 512, :] = grad
                if send_rows:
                    term = lax.dot_general(grad, ch, NT, preferred_element_type=F32)
                    if h == 0:
                        held[g] = term
                    else:
                        send[4 * g : 4 * g + 4] = (held[g] + term).reshape(4, 128, 512).astype(BF16)
                else:
                    term = lax.dot_general(wg, grad, TN, preferred_element_type=F32)
                    if g == 0:
                        held[h] = term
                    else:
                        send[:, h * 64 : h * 64 + 64, :] = (held[h] + term).reshape(8, 64, 512).astype(BF16)

    @pl.when(role == W_ROLE)
    def _():
        body(own, other, False)

    @pl.when(role != W_ROLE)
    def _():
        body(other, own, True)


def row_grad(w, c, grads, out):
    for g in range(2):
        total = jnp.zeros((512, 512), F32)
        for h in range(2):
            ch = c[:, h * 64 : h * 64 + 64, :].reshape(512, 512)
            total += lax.dot_general(grads[h, g * 512 : g * 512 + 512, :], ch, NT, preferred_element_type=F32)
        out[4 * g : 4 * g + 4] = total.reshape(4, 128, 512).astype(out.dtype)


def col_grad(w, c, grads, out):
    w_all = w[...].reshape(1024, 512)
    for h in range(2):
        total = lax.dot_general(w_all, grads[h], TN, preferred_element_type=F32)
        out[:, h * 64 : h * 64 + 64, :] = total.reshape(8, 64, 512).astype(out.dtype)


def front(here, done, gathered, factors, lr, lc, log_total):
    first = log_total is None
    args = [here, done, *gathered, *factors, lr, lc] + ([] if first else [log_total])
    shape = (8, 128, 512)
    out_shape = [pltpu.VMEM(s, BF16) for s in (shape, shape, (2, 1024, 512), shape)]
    if first:
        out_shape.append(pltpu.VMEM((8, 512), F32))
    return vmem_kernel(
        functools.partial(front_kernel, first),
        16,
        in_specs=[IN_SMEM] + [IN_VMEM] * (len(args) - 1),
        out_specs=[IN_VMEM] * len(out_shape),
        out_shape=out_shape,
        cost_estimate=pl.CostEstimate(flops=3 * 10**9, bytes_accessed=16 * 2**20, transcendentals=2**20),
        name="cell_grads",
    )(*args)


def back_kernel(here, w, c, grads, keep):
    role, _, _ = place(here)

    @pl.when(role == W_ROLE)
    def _():
        row_grad(w, c, grads, keep)

    @pl.when(role != W_ROLE)
    def _():
        col_grad(w, c, grads, keep)


def back(here, w, c, grads):
    return vmem_kernel(
        back_kernel,
        12,
        in_specs=[IN_SMEM] + [IN_VMEM] * 3,
        out_specs=IN_VMEM,
        out_shape=pltpu.VMEM(w.shape, F32),
        cost_estimate=pl.CostEstimate(flops=10**9, bytes_accessed=8 * 2**20, transcendentals=0),
        name="own_products",
    )(here, w, c, grads)


def merge_kernel(here, keep, extra, *outs):
    at, _ = own_place(here)
    for k, out in enumerate(outs):
        block = pl.ds(2 * ((at + k) & 3), 2)
        out[...] = (keep[block] + extra[block].astype(F32)).astype(BF16)


def merge(here, keep, extra):
    return vmem_kernel(
        merge_kernel,
        8,
        in_specs=[IN_SMEM] + [IN_VMEM] * 2,
        out_specs=[IN_VMEM] * 4,
        out_shape=[pltpu.VMEM((2, 128, 512), BF16)] * 4,
        name="core_sum",
    )(here, keep, extra)


def ring_sum_kernel(last, here, *refs):
    terms, outs = refs[:4], refs[-2:]
    _, side = own_place(here)

    def total(s):
        out = terms[0][s].astype(F32)
        for term in terms[1:4]:
            out += term[s].astype(F32)
        return out

    mine, theirs = outs
    if last:
        mine[...] = total(side)
        theirs[...] = total(1 - side).astype(BF16)
    else:
        for s in range(2):
            mine[s] = total(s)
            theirs[s] = mine[s].astype(BF16)


def ring_sum(here, terms, last, *after):
    shape = (128, 512) if last else (2, 128, 512)
    return vmem_kernel(
        functools.partial(ring_sum_kernel, last),
        8,
        in_specs=[IN_SMEM] + [IN_VMEM] * (4 + len(after)),
        out_specs=[IN_VMEM] * 2,
        out_shape=[pltpu.VMEM(shape, F32), pltpu.VMEM(shape, BF16)],
        name="ring_sum",
    )(here, *terms, *after)


def pair_kernel(here, mine, far, done, out):
    _, side = own_place(here)
    out[side] = mine[...]
    out[1 - side] = far[...]


def pair(here, mine, far, done):
    return vmem_kernel(
        pair_kernel,
        4,
        in_specs=[IN_SMEM] + [IN_VMEM] * 3,
        out_specs=IN_VMEM,
        out_shape=pltpu.VMEM((2, *mine.shape), BF16),
        name="both_sides",
    )(here, mine, far, done)


def update_kernel(mine, theirs, embed, new):
    new[...] = embed[...] - RATE * (mine[...] + theirs[...].astype(F32))


def update(mine, theirs, embed):
    return vmem_kernel(
        update_kernel,
        4,
        in_specs=[IN_VMEM] * 3,
        out_specs=IN_VMEM,
        out_shape=pltpu.VMEM(embed.shape, F32),
        name="update",
    )(mine, theirs, embed)


def update_both_kernel(here, mine, theirs, embed, far, done, new, payload):
    _, side = own_place(here)

    def fresh(s, old):
        return old[...] - RATE * (mine[s] + theirs[s].astype(F32))

    new[...] = fresh(side, embed)
    payload[side] = new[...].astype(BF16)
    payload[1 - side] = fresh(1 - side, far).astype(BF16)


def update_both(here, mine, theirs, embed, far, done):
    return vmem_kernel(
        update_both_kernel,
        8,
        in_specs=[IN_SMEM] + [IN_VMEM] * 5,
        out_specs=[IN_VMEM] * 2,
        out_shape=[pltpu.VMEM(embed.shape, F32), pltpu.VMEM(mine.shape, BF16)],
        name="update",
    )(here, mine, theirs, embed, far, done)


def prep_kernel(here, row_embed, col_embed, row_marginals, col_marginals, embed, payload, lr, lc, rows, cols, sem):
    row_copy = pltpu.make_async_copy(row_marginals, rows, sem.at[0])
    col_copy = pltpu.make_async_copy(col_marginals, cols, sem.at[3])
    row_copy.start()
    col_copy.start()

    @pl.when(place(here)[0] == W_ROLE)
    def _():
        copy = pltpu.make_async_copy(row_embed, embed, sem.at[1])
        copy.start()
        copy.wait()

    @pl.when(place(here)[0] != W_ROLE)
    def _():
        low = pltpu.make_async_copy(col_embed.at[:, pl.ds(0, 512)], embed.at[pl.ds(0, 64)], sem.at[1])
        high = pltpu.make_async_copy(col_embed.at[:, pl.ds(512, 512)], embed.at[pl.ds(64, 64)], sem.at[2])
        low.start()
        high.start()
        low.wait()
        high.wait()

    row_copy.wait()
    col_copy.wait()
    mine = embed[...].astype(BF16)
    row_values = rows[...].astype(F32)
    rest = jnp.sum(row_values, axis=(0, 1), keepdims=True)
    line = lax.broadcasted_iota(jnp.int32, (8, 512), 0)
    extra = jnp.zeros((8, 512), F32)
    for k in range(3):
        piece = rest.astype(BF16).astype(F32)
        extra = jnp.where(line == k, piece, extra)
        rest = rest - piece
    payload[:128, :] = mine
    payload[128:, :] = extra.astype(BF16)
    log_rows = jnp.log(row_values)
    log_cols = jnp.log(cols[...].astype(F32))
    for k in range(8):
        lr[k * 128 : k * 128 + 128, :] = jnp.broadcast_to(log_rows[k : k + 1, :], (128, 128)).T
    for h in range(2):
        lc[h] = jnp.concatenate([log_cols[4 * h + k : 4 * h + k + 1, :] for k in range(4)], axis=1)


def prep(here, row_embed, col_embed, row_marginals, col_marginals):
    return vmem_kernel(
        prep_kernel,
        4,
        in_specs=[IN_SMEM] + [IN_HBM] * 4,
        out_specs=[IN_VMEM] * 4,
        out_shape=[
            pltpu.VMEM((128, 512), F32),
            pltpu.VMEM((136, 512), BF16),
            pltpu.VMEM((1024, 128), F32),
            pltpu.VMEM((2, 1, 512), F32),
        ],
        scratch_shapes=[pltpu.VMEM((8, 128), jnp.int32)] * 2 + [pltpu.SemaphoreType.DMA((4,))],
        name="first_payload",
    )(here, row_embed, col_embed, row_marginals.reshape(8, 128), col_marginals.reshape(8, 128))


def finish_kernel(here, embed, theirs, new_row, new_col, sem):
    def write(row, col):
        copies = [
            pltpu.make_async_copy(row, new_row, sem.at[0]),
            pltpu.make_async_copy(col.at[pl.ds(0, 64)], new_col.at[:, pl.ds(0, 512)], sem.at[1]),
            pltpu.make_async_copy(col.at[pl.ds(64, 64)], new_col.at[:, pl.ds(512, 512)], sem.at[2]),
        ]
        for copy in copies:
            copy.start()
        for copy in copies:
            copy.wait()

    @pl.when(place(here)[0] == W_ROLE)
    def _():
        write(embed, theirs)

    @pl.when(place(here)[0] != W_ROLE)
    def _():
        write(theirs, embed)


def finish(here, embed, theirs):
    return vmem_kernel(
        finish_kernel,
        4,
        in_specs=[IN_SMEM, IN_VMEM, IN_VMEM],
        out_specs=[IN_HBM] * 2,
        out_shape=[pltpu.HBM((128, 512), F32), pltpu.HBM((64, 1024), F32)],
        scratch_shapes=[pltpu.SemaphoreType.DMA((3,))],
        name="results",
    )(here, embed, theirs)


def per_device(swap, across, along, row_embed, col_embed, counts, block_rows, block_cols, row_marginals, col_marginals):
    here = lax.axis_index(AXES).astype(jnp.int32).reshape(1)
    steps = counts.shape[0]

    def other_core(x):
        return lax.ppermute(x, "rep", swap)

    def other_side(x):
        return lax.ppermute(x, AXES, across)

    def ring(x, k):
        return lax.ppermute(x, AXES, along[k])

    embed, payload, lr, lc = prep(here, row_embed, col_embed, row_marginals, col_marginals)
    rows = block_rows.reshape(steps, 1, -1)
    cols = block_cols.reshape(steps, 1, -1)

    low, done = abn(counts, rows, cols, 0, 0, payload)
    payload = pair(here, payload, other_side(payload), done)
    log_total = None
    for step in range(steps):
        last = step + 1 == steps
        got = {k: ring(payload, k) for k in (2, 1, 3)}
        if step == 0:
            high, done = abn(counts, rows, cols, 0, 1, payload)
            got[3], done = lax.optimization_barrier((got[3], done))
        own = [payload, got[1], got[2], got[3]]
        other = [other_core(x) for x in own]
        res = front(here, done, own + other, low + high, lr, lc, log_total)
        if step == 0:
            *res, log_total = res
        w, c, grads, send = res
        extra = other_core(send)
        keep = back(here, w, c, grads)
        terms = merge(here, keep, extra)
        if not last:
            embed, *terms = lax.optimization_barrier((embed, *terms))
        got = {k: ring(terms[k], k) for k in (2, 1, 3)}
        terms = [terms[0], got[1], got[2], got[3]]
        if last:
            mine, theirs = ring_sum(here, terms, last)
            embed = update(mine, other_side(theirs), embed)
        else:
            far = other_side(embed)
            low, done = abn(counts, rows, cols, step + 1, 0, terms[0])
            mine, theirs = ring_sum(here, terms, last, done)
            high, done = abn(counts, rows, cols, step + 1, 1, theirs)
            embed, payload = update_both(here, mine, other_side(theirs), embed, far, done)
    return tuple(finish(here, embed, other_core(embed)))


def solution(mesh):
    n_row, n_col = mesh.shape["row"], mesh.shape["col"]
    across, along = [], {1: [], 2: [], 3: []}
    for r in range(n_row):
        for c in range(n_col):
            for p in range(2):
                i = (r * n_col + c) * 2 + p
                if p == W_ROLE:
                    across.append((i, (r * n_col + (c ^ 1)) * 2 + p))
                    for k in along:
                        along[k].append((i, (r * n_col + (c + 2 * k) % n_col) * 2 + p))
                else:
                    across.append((i, ((r ^ 1) * n_col + c) * 2 + p))
                    for k in along:
                        along[k].append((i, ((r + 2 * k) % n_row * n_col + c) * 2 + p))
    swap = [(0, 1), (1, 0)]
    return jax.shard_map(
        functools.partial(per_device, swap, across, along),
        mesh=mesh,
        in_specs=(
            P(("row", "col"), None),
            P("row", "col"),
            P(None, "rep", "row", "col"),
            P(None, "rep", "row", "col"),
            P(None, "rep", "row", "col"),
            P("row"),
            P("col"),
        ),
        out_specs=(P(("row", "col"), None), P("row", "col")),
        check_vma=False,
    )
```
